256 devices in a mesh: pb: 16 (over x_hi, y, core), ka: 16 (over x_lo, z).
Axes of the slice: x: 4 (x_hi: 2, x_lo: 2; x = x_hi * 2 + x_lo), y: 4, z: 8, core: 2. Of those that a mesh axis runs over, the one named last changes fastest.
Arguments:
- query: float32 [32768, 128], P(('pb', 'ka')), may hold values from -6 to 6
- keys: float32 [32768, 128], P(('ka', 'pb')), may hold values from -6 to 6
- values: float32 [32768, 128], P(('ka', 'pb')), may hold values from -6 to 6
- attn_out: float32 [32768, 128], P(('pb', 'ka')), may hold values from -6 to 6
- out_grad: float32 [32768, 128], P(('pb', 'ka')), may hold values from -6 to 6
- row_lse: float32 [1, 32768], P(None, ('pb', 'ka')), may hold values from 5 to 7
Outputs:
- query_grad: float32 [32768, 128], P(('pb', 'ka'))
- key_grad: float32 [32768, 128], P(('ka', 'pb'))
- value_grad: float32 [32768, 128], P(('ka', 'pb'))
The draws below stay inside these ranges and needn't reach their ends.
All inputs are finite; a program needn't handle non-finite values.
Results may differ from the reference program's by a relative error of at most 0.0003.
Values sent between devices are 32-bit elements; how exact they have to be, the bound alone decides.
No kernel may reach another device: no remote copies, remote signals or barrier semaphores. Data moves between devices by JAX's collectives and lax.ppermute only.
A program may use at most 128 MiB of HBM per device.

```python
import math
import jax
import jax.numpy as jnp
from jax import lax

D_HEAD = 128
HEADS = 1
TOKENS = 32768
QB = 2048


def block_levels(key, shape, cuts, smallest, top_value):
    loudness = 1.0
    for axis_at, parts in cuts:
        steps = jax.random.uniform(jax.random.fold_in(jax.random.fold_in(key, 6), axis_at), (parts,), jnp.float32, smallest / len(cuts), top_value / len(cuts))
        loudness = loudness * jnp.repeat(jnp.exp(steps), shape[axis_at] // parts).reshape((-1,) + (1,) * (len(shape) - 1 - axis_at))
    return loudness


def centred(key, dims, spread, limit, pieces=(), kind=jnp.bfloat16):
    result = spread * jax.random.normal(key, dims, jnp.float32)
    if pieces:
        result = result * block_levels(key, dims, pieces, -0.22, 0.18)
    return jnp.clip(result, -limit, limit).astype(kind)


def setup_inputs(seed: int = 0) -> dict:
    key_of = jax.random.split(jax.random.key(seed), 7)
    query = centred(key_of[0], (TOKENS, HEADS * D_HEAD), 1.0, 6.0, ((0, 256),), jnp.float32)
    keys = centred(key_of[1], (TOKENS, HEADS * D_HEAD), 1.0, 6.0, ((0, 256),), jnp.float32)
    values = centred(key_of[2], (TOKENS, HEADS * D_HEAD), 1.0, 6.0, ((0, 256),), jnp.float32)
    attn_out = centred(key_of[3], (TOKENS, HEADS * D_HEAD), 1.0, 6.0, ((0, 256),), jnp.float32)
    out_grad = centred(key_of[4], (TOKENS, HEADS * D_HEAD), 1.0, 6.0, ((0, 256),), jnp.float32)
    row_lse = jnp.clip(5.0 + 2.0 * jax.random.uniform(key_of[5], (HEADS, TOKENS), jnp.float32) ** block_levels(key_of[5], (HEADS, TOKENS), ((1, 256),), -0.2, 0.2), 5.0, 7.0)
    return {"query": query, "keys": keys, "values": values, "attn_out": attn_out, "out_grad": out_grad, "row_lse": row_lse}


def dot_full(a, b):
    return jnp.dot(a, b, precision=lax.Precision.HIGHEST, preferred_element_type=jnp.float32)

def head_grads(q_head, k_head, v_head, g_head, lse_head, delta_head):
    scale = 1.0 / math.sqrt(D_HEAD)
    blocks = TOKENS // QB
    q_blocks = q_head.reshape(blocks, QB, D_HEAD)
    g_blocks = g_head.reshape(blocks, QB, D_HEAD)
    l_blocks = lse_head.reshape(blocks, QB)
    d_blocks = delta_head.reshape(blocks, QB)

    def step(carry, items):
        k_acc, v_acc = carry
        q_blk, g_blk, l_blk, d_blk = items
        scores = dot_full(q_blk, k_head.T) * scale
        probs = jnp.exp(scores - l_blk[:, None])
        dprob = dot_full(g_blk, v_head.T)
        dscore = probs * (dprob - d_blk[:, None])
        q_grad = dot_full(dscore, k_head) * scale
        k_acc = k_acc + dot_full(dscore.T, q_blk) * scale
        v_acc = v_acc + dot_full(probs.T, g_blk)
        return ((k_acc, v_acc), q_grad)
    zeros = jnp.zeros((TOKENS, D_HEAD), jnp.float32)
    (k_grad, v_grad), q_grads = lax.scan(step, (zeros, zeros), (q_blocks, g_blocks, l_blocks, d_blocks))
    return (q_grads.reshape(TOKENS, D_HEAD), k_grad, v_grad)

def reference(query, keys, values, attn_out, out_grad, row_lse):
    delta = lax.optimization_barrier(jnp.sum((out_grad * attn_out).reshape(TOKENS, HEADS, D_HEAD), axis=-1)).T
    q_list, k_list, v_list = ([], [], [])
    for head in range(HEADS):
        cols = slice(head * D_HEAD, (head + 1) * D_HEAD)
        q_g, k_g, v_g = head_grads(query[:, cols], keys[:, cols], values[:, cols], out_grad[:, cols], row_lse[head], delta[head])
        q_list.append(q_g)
        k_list.append(k_g)
        v_list.append(v_g)
    return (jnp.concatenate(q_list, axis=1), jnp.concatenate(k_list, axis=1), jnp.concatenate(v_list, axis=1))
```

```python
import functools
import math

import jax
import jax.numpy as jnp
from jax import lax
from jax.experimental import pallas as pl
from jax.experimental.pallas import tpu as pltpu
from jax.sharding import Mesh, PartitionSpec as P

D = 128
SCALE = 1.0 / math.sqrt(D)
LOG2E = math.log2(math.e)
LN2 = math.log(2.0)
BF16 = jnp.bfloat16
F32 = jnp.float32

AXES = ("xh", "y", "c", "xl", "z")
PLANE = ("xh", "y", "xl")
COLUMN = ("c", "z")
ROWS = 128
BLOCKS = 16
TOKENS = ROWS * BLOCKS
PACK = 2 * ROWS + 8
KEY_BLOCKS = 4
TK = KEY_BLOCKS * ROWS
TQ = 512


def split(x):
    high = x.astype(BF16)
    return high, (x - high.astype(F32)).astype(BF16)


def split3(x):
    a = x.astype(BF16)
    rest = x - a.astype(F32)
    b = rest.astype(BF16)
    return a, b, (rest - b.astype(F32)).astype(BF16)


def dot(a, b):
    return jnp.dot(a, b, preferred_element_type=F32)


def load_queries(qg_ref, base, factor, row_at, row_factor, turned, wide, narrow):
    zeros = jnp.zeros((ROWS, ROWS), BF16)
    sub = lax.broadcasted_iota(jnp.int32, (ROWS, ROWS), 0)
    for b in range(BLOCKS):
        at = slice(b * ROWS, (b + 1) * ROWS)
        x = qg_ref[b, base : base + ROWS, :] * factor
        high, low = split(x)
        wide[at, :ROWS] = high
        wide[at, ROWS:] = low
        narrow[at, :ROWS] = high
        narrow[at, ROWS:] = zeros
        high, low = split(x.T)
        turned[:ROWS, at] = high
        turned[ROWS : 2 * ROWS, at] = low
        turned[2 * ROWS : 3 * ROWS, at] = high
        first, second, third = split3(qg_ref[b, row_at : row_at + 1, :] * -row_factor)
        tail = jnp.where(
            sub == 0,
            first.astype(F32),
            jnp.where(sub == 1, second.astype(F32), jnp.where(sub == 2, third.astype(F32), 0.0)),
        )
        turned[3 * ROWS :, at] = tail.astype(BF16)


def tile_kernel(
    core_ref, qg_ref, kv_ref, dq_ref, theirs_ref, mine_ref, qt, gt, q_wide, q_narrow, g_wide, g_narrow, dqt
):
    step = pl.program_id(0)
    steps = BLOCKS // KEY_BLOCKS

    @pl.when(step == 0)
    def _():
        load_queries(qg_ref, 0, SCALE * LOG2E, 2 * ROWS, LOG2E, qt, q_wide, q_narrow)
        load_queries(qg_ref, ROWS, 1.0, 2 * ROWS + 1, 1.0, gt, g_wide, g_narrow)
        dqt[...] = jnp.zeros_like(dqt)

    ones = (lax.broadcasted_iota(jnp.int32, (TK, ROWS), 1) < 3).astype(F32).astype(BF16)
    k = kv_ref[:, :ROWS, :].reshape(TK, D)
    v = kv_ref[:, ROWS:, :].reshape(TK, D)
    k_high, k_low = split(k)
    v_high, v_low = split(v)
    k_all = jnp.concatenate([k_high, k_high, k_low, ones], 1)
    v_all = jnp.concatenate([v_high, v_high, v_low, ones], 1)
    kt_high, kt_low = split(k.T)
    kt_both = jnp.concatenate([kt_high, kt_low], 0)
    dv = jnp.zeros((TK, 2 * D), F32)
    dk = jnp.zeros((TK, 2 * D), F32)
    for j in range(TOKENS // TQ):
        at = slice(j * TQ, (j + 1) * TQ)
        probs = jnp.exp2(dot(k_all, qt[:, at]))
        dprob = dot(v_all, gt[:, at])
        high, low = split(probs)
        dv += dot(high, g_wide[at, :]) + dot(low, g_narrow[at, :])
        high, low = split(probs * dprob)
        dk += dot(high, q_wide[at, :]) + dot(low, q_narrow[at, :])
        part = dot(kt_both, high)
        dqt[:, at] = dqt[:, at] + (part[:D] + part[D:] + dot(kt_high, low))
    dk = (dk[:, :D] + dk[:, D:]) * LN2
    dv = dv[:, :D] + dv[:, D:]

    def store(ref):
        ref[:, :ROWS, :] = dk.reshape(KEY_BLOCKS, ROWS, D)
        ref[:, ROWS:, :] = dv.reshape(KEY_BLOCKS, ROWS, D)

    @pl.when(step < steps // 2)
    def _():
        store(theirs_ref)

    @pl.when(step >= steps // 2)
    def _():
        store(mine_ref)

    @pl.when(step == steps - 1)
    def _():
        for b in range(BLOCKS):
            dq_ref[b] = (dqt[:, b * ROWS : (b + 1) * ROWS] * SCALE).T


def tile_grads(core, qg, kv):
    steps = BLOCKS // KEY_BLOCKS
    half = steps // 2
    block = (KEY_BLOCKS, 2 * ROWS, D)
    grid_spec = pltpu.PrefetchScalarGridSpec(
        num_scalar_prefetch=1,
        grid=(steps,),
        in_specs=[
            pl.BlockSpec((BLOCKS, PACK, D), lambda i, c: (0, 0, 0)),
            pl.BlockSpec(block, lambda i, c: ((i + half * (1 - c[0])) % steps, 0, 0)),
        ],
        out_specs=[
            pl.BlockSpec((BLOCKS, ROWS, D), lambda i, c: (0, 0, 0)),
            pl.BlockSpec(block, lambda i, c: (jnp.minimum(i, half - 1), 0, 0)),
            pl.BlockSpec(block, lambda i, c: (jnp.maximum(i - half, 0), 0, 0)),
        ],
        scratch_shapes=[pltpu.VMEM((4 * ROWS, TOKENS), BF16)] * 2
        + [pltpu.VMEM((TOKENS, 2 * D), BF16)] * 4
        + [pltpu.VMEM((D, TOKENS), F32)],
    )
    return pl.pallas_call(
        tile_kernel,
        grid_spec=grid_spec,
        out_shape=[
            jax.ShapeDtypeStruct((BLOCKS, ROWS, D), F32),
            jax.ShapeDtypeStruct((BLOCKS // 2, 2 * ROWS, D), F32),
            jax.ShapeDtypeStruct((BLOCKS // 2, 2 * ROWS, D), F32),
        ],
        compiler_params=pltpu.CompilerParams(vmem_limit_bytes=48 * 1024 * 1024),
        cost_estimate=pl.CostEstimate(flops=20 * 2 * TOKENS * TOKENS * D, bytes_accessed=8 << 20, transcendentals=TOKENS * TOKENS),
    )(core, qg, kv)


def on_device(query, keys, values, attn_out, out_grad, row_lse):
    delta = jnp.sum(out_grad * attn_out, axis=-1)[None, :]
    pack = jnp.concatenate([query, out_grad, row_lse, delta, jnp.zeros((6, D), F32)], 0)
    kv = lax.all_gather(jnp.concatenate([keys, values], 0)[None], COLUMN, axis=0, tiled=True)
    qg = lax.all_to_all(jnp.broadcast_to(pack[None], (BLOCKS, PACK, D)), PLANE, 0, 0)
    core = lax.axis_index("c")
    dq, theirs, mine = tile_grads(core.astype(jnp.int32)[None], qg, kv)
    dkv = mine + lax.ppermute(theirs, "c", [(0, 1), (1, 0)])
    dkv = lax.psum_scatter(dkv, "z", scatter_dimension=0, tiled=True)
    dq = jnp.sum(lax.all_to_all(dq, PLANE, 0, 0), axis=0)
    return dq, dkv[0, :ROWS], dkv[0, ROWS:]


def solution(mesh):
    fine = Mesh(mesh.devices.reshape(2, 4, 2, 2, 8), AXES)
    rows = P(("xh", "y", "c", "xl", "z"), None)
    cols = P(("xl", "z", "xh", "y", "c"), None)
    return jax.shard_map(
        on_device,
        mesh=fine,
        in_specs=(rows, cols, cols, rows, rows, P(None, ("xh", "y", "c", "xl", "z"))),
        out_specs=(rows, cols, cols),
        check_vma=False,
    )
```

```python
import math

import jax
import jax.numpy as jnp
from jax import lax
from jax.experimental import pallas as pl
from jax.experimental.pallas import tpu as pltpu
from jax.sharding import Mesh, PartitionSpec as P

D = 128
SCALE = 1.0 / math.sqrt(D)
LOG2E = math.log2(math.e)
LN2 = math.log(2.0)
BF16 = jnp.bfloat16
F32 = jnp.float32

AXES = ("xh", "y", "c", "xl", "z")
PLANE = ("xh", "y", "xl")
COLUMN = ("c", "z")
DEPTH = 8
ROWS = 128
HALF = ROWS // 2
BLOCKS = 16
TOKENS = ROWS * BLOCKS
PACK = 2 * ROWS + 8
CHUNKS = 4
TQ = TOKENS // CHUNKS
TK = BLOCKS * HALF

SWAP = [(0, 1), (1, 0)]


def shape(*dims, dtype=F32):
    return jax.ShapeDtypeStruct(dims, dtype)


def split(x):
    high = x.astype(BF16)
    return high, (x - high.astype(F32)).astype(BF16)


def split3(x):
    a = x.astype(BF16)
    rest = x - a.astype(F32)
    b = rest.astype(BF16)
    return a, b, (rest - b.astype(F32)).astype(BF16)


def dot(a, b):
    return jnp.dot(a, b, preferred_element_type=F32)


def pack_kernel(q, k, v, o, g, lse, own, copies):
    own[:ROWS] = q[...]
    own[ROWS : 2 * ROWS] = g[...]
    delta = jnp.sum((g[...] * o[...]).T, axis=0, keepdims=True)
    own[2 * ROWS :] = jnp.concatenate([lse[...], delta, jnp.zeros((6, D), F32)], 0)
    for b in range(BLOCKS):
        copies[b, :HALF] = k[:HALF]
        copies[b, HALF : 2 * HALF] = v[:HALF]
        copies[b, 2 * HALF : 3 * HALF] = k[HALF:]
        copies[b, 3 * HALF :] = v[HALF:]


def pack(query, keys, values, attn_out, out_grad, row_lse):
    return pl.pallas_call(pack_kernel, out_shape=[shape(PACK, D), shape(BLOCKS, 2 * ROWS, D)])(
        query, keys, values, attn_out, out_grad, row_lse
    )


def load_block(x_ref, base, factor, row_at, row_factor, at, turned, wide):
    x = x_ref[base : base + ROWS, :] * factor
    high, low = split(x)
    wide[at, :D] = high
    wide[at, D:] = low
    high, low = split(x.T)
    turned[:D, at] = high
    turned[D : 2 * D, at] = low
    turned[2 * D : 3 * D, at] = high
    a, b, c = split3(x_ref[row_at : row_at + 1, :] * -row_factor)
    sub = lax.broadcasted_iota(jnp.int32, (D, ROWS), 0)
    tail = jnp.where(sub == 0, a.astype(F32), jnp.where(sub == 1, b.astype(F32), jnp.where(sub == 2, c.astype(F32), 0.0)))
    turned[3 * D :, at] = tail.astype(BF16)


def tile_kernel(*refs):
    packs, kv_ref, mine, theirs, dkv_ref = refs[:BLOCKS], *refs[BLOCKS : BLOCKS + 4]
    qt, gt, q_wide, g_wide = refs[BLOCKS + 4 : BLOCKS + 8]
    ones = (lax.broadcasted_iota(jnp.int32, (TK, D), 1) < 3).astype(F32).astype(BF16)
    k = kv_ref[:, :HALF, :].reshape(TK, D)
    v = kv_ref[:, HALF:, :].reshape(TK, D)
    k_high, k_low = split(k)
    v_high, v_low = split(v)
    k_all = jnp.concatenate([k_high, k_high, k_low, ones], 1)
    v_all = jnp.concatenate([v_high, v_high, v_low, ones], 1)
    kt_high, kt_low = split(k.T)
    kt_both = jnp.concatenate([kt_high, kt_low], 0)
    dv = jnp.zeros((TK, 2 * D), F32)
    dk = jnp.zeros((TK, 2 * D), F32)
    for j in range(CHUNKS):
        for b in range(4 * j, 4 * j + 4):
            at = slice(b * ROWS, (b + 1) * ROWS)
            load_block(packs[b], 0, SCALE * LOG2E, 2 * ROWS, LOG2E, at, qt, q_wide)
            load_block(packs[b], ROWS, 1.0, 2 * ROWS + 1, 1.0, at, gt, g_wide)
        at = slice(j * TQ, (j + 1) * TQ)
        probs = jnp.exp2(dot(k_all, qt[:, at]))
        dprob = dot(v_all, gt[:, at])
        high, low = split(probs)
        dv += dot(high, g_wide[at, :]) + dot(low, g_wide[at, :])
        high, low = split(probs * dprob)
        dk += dot(high, q_wide[at, :]) + dot(low, q_wide[at, :])
        part = dot(kt_both, high)
        part = (part[:D] + part[D:] + dot(kt_high, low)) * SCALE
        for b in range(2):
            mine[j, b] = part[:, b * ROWS : (b + 1) * ROWS].T
            theirs[j, b] = part[:, (b + 2) * ROWS : (b + 3) * ROWS].T
    dkv_ref[:, :HALF, :] = ((dk[:, :D] + dk[:, D:]) * LN2).reshape(BLOCKS, HALF, D)
    dkv_ref[:, HALF:, :] = (dv[:, :D] + dv[:, D:]).reshape(BLOCKS, HALF, D)


def tile_grads(packs, kv, at):
    half = (CHUNKS, 2, ROWS, D)
    return pl.pallas_call(
        tile_kernel,
        grid=(1,),
        in_specs=[pl.BlockSpec((PACK, D), lambda i: (0, 0))] * BLOCKS + [pl.BlockSpec((BLOCKS, ROWS, D), lambda i: (0, at, 0))],
        out_specs=[
            pl.BlockSpec(half, lambda i: (0, 0, 0, 0)),
            pl.BlockSpec(half, lambda i: (0, 0, 0, 0)),
            pl.BlockSpec((BLOCKS, ROWS, D), lambda i: (0, 0, 0)),
        ],
        out_shape=[shape(*half), shape(*half), shape(BLOCKS, ROWS, D)],
        scratch_shapes=[pltpu.VMEM((4 * D, TOKENS), BF16)] * 2 + [pltpu.VMEM((TOKENS, 2 * D), BF16)] * 2,
        compiler_params=pltpu.CompilerParams(vmem_limit_bytes=32 * 1024 * 1024),
        cost_estimate=pl.CostEstimate(flops=12_000_000_000, bytes_accessed=8 << 20, transcendentals=TOKENS * TK),
    )(*packs, kv)


def swap(x):
    return lax.ppermute(x, "c", SWAP)


def along(x, step):
    pairs = [(z, (z + step) % DEPTH) for z in range(DEPTH)]
    pairs += [(DEPTH + z, DEPTH + (z - step) % DEPTH) for z in range(DEPTH)]
    return lax.ppermute(x, COLUMN, pairs)


def on_device(query, keys, values, attn_out, out_grad, row_lse):
    own, kv = pack(query, keys, values, attn_out, out_grad, row_lse)
    kv = lax.all_to_all(kv, PLANE, 0, 0)
    other = swap(own)
    a, b = own, other
    packs = []
    for j in range(1, CHUNKS):
        a, b = along(a, 1), along(b, 1)
        packs += [swap(b), swap(a), b, a]
    far = along(a, 1)
    packs = [own, far, other, swap(far)] + packs
    packs = [pltpu.with_memory_space_constraint(x, pltpu.HBM) for x in packs]
    kv = pltpu.with_memory_space_constraint(kv, pltpu.HBM)
    mine1, theirs1, dkv1 = tile_grads(packs, kv, 0)
    dkv1 = lax.all_to_all(dkv1, PLANE, 0, 0)
    mine2, theirs2, dkv2 = tile_grads(packs, kv, 1)
    theirs2, dkv1 = lax.optimization_barrier((theirs2, dkv1))
    dq = (mine1 + swap(theirs1)) + (mine2 + swap(theirs2))
    r1 = along(dq[1], 1)
    r2 = along(dq[2], 2)
    r3 = along(dq[3], 3)
    r4 = along(dq[0, 1], 4)
    dkv2 = lax.all_to_all(dkv2, PLANE, 0, 0)
    r1, r2, r3, r4, dkv2 = lax.optimization_barrier((r1, r2, r3, r4, dkv2))
    query_grad = (dq[0, 0] + r4) + (r1[0] + r2[0] + r3[0]) + swap(r1[1] + r2[1] + r3[1])
    s1 = jnp.sum(dkv1, axis=0)
    s2 = jnp.sum(dkv2, axis=0)
    key_grad = jnp.concatenate([s1[:HALF], s2[:HALF]], 0)
    value_grad = jnp.concatenate([s1[HALF:], s2[HALF:]], 0)
    return query_grad, key_grad, value_grad


def solution(mesh):
    fine = Mesh(mesh.devices.reshape(2, 4, 2, 2, DEPTH), AXES)
    rows = P(("xh", "y", "c", "xl", "z"), None)
    cols = P(("xl", "z", "xh", "y", "c"), None)
    return jax.shard_map(
        on_device,
        mesh=fine,
        in_specs=(rows, cols, cols, rows, rows, P(None, ("xh", "y", "c", "xl", "z"))),
        out_specs=(rows, cols, cols),
        check_vma=False,
    )
```

```python
import math

import jax
import jax.numpy as jnp
from jax import lax
from jax.experimental import pallas as pl
from jax.experimental.pallas import tpu as pltpu
from jax.sharding import Mesh, PartitionSpec as P

D = 128
SCALE = 1.0 / math.sqrt(D)
LOG2E = math.log2(math.e)
LN2 = math.log(2.0)
BF16 = jnp.bfloat16
F32 = jnp.float32

AXES = ("xh", "y", "c", "xl", "z")
PLANE = ("xh", "y", "xl")
COLUMN = ("c", "z")
DEPTH = 8
ROWS = 128
BLOCKS = 16
TOKENS = ROWS * BLOCKS
PACK = 2 * ROWS + 8
CHUNKS = 4
TQ = TOKENS // CHUNKS
TK = TOKENS // 2

SWAP = [(0, 1), (1, 0)]


def shape(*dims, dtype=F32):
    return jax.ShapeDtypeStruct(dims, dtype)


def split(x):
    high = x.astype(BF16)
    return high, (x - high.astype(F32)).astype(BF16)


def split3(x):
    a = x.astype(BF16)
    rest = x - a.astype(F32)
    b = rest.astype(BF16)
    return a, b, (rest - b.astype(F32)).astype(BF16)


def dot(a, b):
    return jnp.dot(a, b, preferred_element_type=F32)


def pack_kernel(k, v, q, o, g, lse, own, copies):
    own[:ROWS] = q[...]
    own[ROWS : 2 * ROWS] = g[...]
    delta = jnp.sum((g[...] * o[...]).T, axis=0, keepdims=True)
    own[2 * ROWS :] = jnp.concatenate([lse[...], delta, jnp.zeros((6, D), F32)], 0)
    for b in range(BLOCKS):
        copies[b, :ROWS] = k[...]
        copies[b, ROWS:] = v[...]


def pack(query, keys, values, attn_out, out_grad, row_lse):
    return pl.pallas_call(pack_kernel, out_shape=[shape(PACK, D), shape(BLOCKS, 2 * ROWS, D)])(
        keys, values, query, attn_out, out_grad, row_lse
    )


def load_block(x_ref, base, factor, row_at, row_factor, at, turned, wide):
    x = x_ref[base : base + ROWS, :] * factor
    high, low = split(x)
    wide[at, :D] = high
    wide[at, D : 2 * D] = high
    wide[at, 2 * D : 3 * D] = low
    high, low = split(x.T)
    turned[:D, at] = high
    turned[D:, at] = low
    a, b, c = split3(x_ref[row_at : row_at + 1, :] * -row_factor)
    sub = lax.broadcasted_iota(jnp.int32, (D, ROWS), 0)
    tail = jnp.where(sub == 0, a.astype(F32), jnp.where(sub == 1, b.astype(F32), jnp.where(sub == 2, c.astype(F32), 0.0)))
    wide[at, 3 * D :] = tail.T.astype(BF16)


def tile_kernel(*refs):
    packs, kv_ref, mine, theirs, dkv_ref = refs[:BLOCKS], *refs[BLOCKS : BLOCKS + 4]
    q_turned, g_turned, q_all, g_all, dq, local, sems = refs[BLOCKS + 4 :]
    step = pl.program_id(0)

    @pl.when(step == 0)
    def _():
        copies = [pltpu.make_async_copy(packs[b], local.at[b], sems.at[b]) for b in range(BLOCKS)]
        for copy in copies:
            copy.start()
        for b in range(BLOCKS):
            copies[b].wait()
            at = slice(b * ROWS, (b + 1) * ROWS)
            load_block(local.at[b], 0, SCALE * LOG2E, 2 * ROWS, LOG2E, at, q_turned, q_all)
            load_block(local.at[b], ROWS, 1.0, 2 * ROWS + 1, 1.0, at, g_turned, g_all)
        dq[...] = jnp.zeros_like(dq)

    ones = (lax.broadcasted_iota(jnp.int32, (D, TK), 0) < 3).astype(F32).astype(BF16)
    k = kv_ref[:, :ROWS, :].reshape(TK, D)
    v = kv_ref[:, ROWS:, :].reshape(TK, D)
    k_high, k_low = split(k.T)
    v_high, v_low = split(v.T)
    k_all = jnp.concatenate([k_high, k_low, k_high, ones], 0)
    v_all = jnp.concatenate([v_high, v_low, v_high, ones], 0)
    k_wide = jnp.concatenate(split(k), 1)
    dvt = jnp.zeros((D, TK), F32)
    dkt = jnp.zeros((D, TK), F32)
    for j in range(TOKENS // TQ):
        at = slice(j * TQ, (j + 1) * TQ)
        probs = jnp.exp2(dot(q_all[at, :], k_all))
        dprob = dot(g_all[at, :], v_all)
        high, low = split(probs)
        part = dot(g_turned[:, at], high)
        dvt += part[:D] + part[D:] + dot(g_turned[:D, at], low)
        high, low = split(probs * dprob)
        part = dot(q_turned[:, at], high)
        dkt += part[:D] + part[D:] + dot(q_turned[:D, at], low)
        part = dot(high, k_wide) + dot(low, k_wide)
        dq[at, :] = dq[at, :] + (part[:, :D] + part[:, D:])
    dkv_ref[:, :ROWS, :] = (dkt * LN2).T.reshape(TK // ROWS, ROWS, D)
    dkv_ref[:, ROWS:, :] = dvt.T.reshape(TK // ROWS, ROWS, D)

    @pl.when(step == pl.num_programs(0) - 1)
    def _():
        for j in range(CHUNKS):
            for b in range(2):
                at = (4 * j + b) * ROWS
                mine[j, b] = dq[at : at + ROWS] * SCALE
                at += 2 * ROWS
                theirs[j, b] = dq[at : at + ROWS] * SCALE


def tile_grads(packs, kv):
    half = (CHUNKS, 2, ROWS, D)
    block = pl.BlockSpec((TK // ROWS, 2 * ROWS, D), lambda i: (i, 0, 0))
    return pl.pallas_call(
        tile_kernel,
        grid=(TOKENS // TK,),
        in_specs=[pl.BlockSpec(memory_space=pl.ANY)] * BLOCKS + [block],
        out_specs=[pl.BlockSpec(half, lambda i: (0, 0, 0, 0))] * 2 + [block],
        out_shape=[shape(*half), shape(*half), pltpu.HBM((BLOCKS, 2 * ROWS, D), F32)],
        scratch_shapes=[pltpu.VMEM((2 * D, TOKENS), BF16)] * 2
        + [pltpu.VMEM((TOKENS, 4 * D), BF16)] * 2
        + [pltpu.VMEM((TOKENS, D), F32), pltpu.VMEM((BLOCKS, PACK, D), F32), pltpu.SemaphoreType.DMA((BLOCKS,))],
        compiler_params=pltpu.CompilerParams(vmem_limit_bytes=36 * 1024 * 1024),
        cost_estimate=pl.CostEstimate(flops=24_000_000_000, bytes_accessed=8 << 20, transcendentals=TOKENS * TOKENS),
    )(*packs, kv)


def swap(x):
    return lax.ppermute(x, "c", SWAP)


def along(x, step):
    pairs = [(z, (z + step) % DEPTH) for z in range(DEPTH)]
    pairs += [(DEPTH + z, DEPTH + (z - step) % DEPTH) for z in range(DEPTH)]
    return lax.ppermute(x, COLUMN, pairs)


def on_device(query, keys, values, attn_out, out_grad, row_lse):
    own, kv = pack(query, keys, values, attn_out, out_grad, row_lse)
    other = swap(own)
    kv = lax.all_to_all(kv, PLANE, 0, 0)
    a, b = own, other
    packs = []
    for j in range(1, CHUNKS):
        a, b = along(a, 1), along(b, 1)
        packs += [swap(b), swap(a), b, a]
    far = along(a, 1)
    packs = [own, far, other, swap(far)] + packs
    packs = [pltpu.with_memory_space_constraint(x, pltpu.HBM) for x in packs]
    mine, theirs, dkv = tile_grads(packs, kv)
    dq = mine + swap(theirs)
    dkv = lax.all_to_all(dkv, PLANE, 0, 0)
    r1 = along(dq[1], 1)
    r2 = along(dq[2], 2)
    r3 = along(dq[3], 3)
    r4 = along(dq[0, 1], 4)
    query_grad = (dq[0, 0] + r4) + (r1[0] + r2[0] + r3[0]) + swap(r1[1] + r2[1] + r3[1])
    query_grad, dkv = lax.optimization_barrier((query_grad, dkv))
    dkv = jnp.sum(dkv, axis=0)
    return query_grad, dkv[:ROWS], dkv[ROWS:]


def solution(mesh):
    fine = Mesh(mesh.devices.reshape(2, 4, 2, 2, DEPTH), AXES)
    rows = P(("xh", "y", "c", "xl", "z"), None)
    cols = P(("xl", "z", "xh", "y", "c"), None)
    return jax.shard_map(
        on_device,
        mesh=fine,
        in_specs=(rows, cols, cols, rows, rows, P(None, ("xh", "y", "c", "xl", "z"))),
        out_specs=(rows, cols, cols),
        check_vma=False,
    )
```

```python
import math

import jax
import jax.numpy as jnp
from jax import lax
from jax.experimental import pallas as pl
from jax.experimental.pallas import tpu as pltpu
from jax.sharding import Mesh, PartitionSpec as P

D = 128
SCALE = 1.0 / math.sqrt(D)
LOG2E = math.log2(math.e)
LN2 = math.log(2.0)
BF16 = jnp.bfloat16
F32 = jnp.float32

AXES = ("xh", "y", "c", "xl", "z")
PLANE = ("xh", "y", "xl")
COLUMN = ("c", "z")
DEPTH = 8
ROWS = 128
BLOCKS = 16
TOKENS = ROWS * BLOCKS
PACK = 2 * ROWS + 8
CHUNKS = 4
TQ = TOKENS // CHUNKS
TK = TOKENS // 2

SWAP = [(0, 1), (1, 0)]


def shape(*dims, dtype=F32):
    return jax.ShapeDtypeStruct(dims, dtype)


def split(x):
    high = x.astype(BF16)
    return high, (x - high.astype(F32)).astype(BF16)


def split3(x):
    a = x.astype(BF16)
    rest = x - a.astype(F32)
    b = rest.astype(BF16)
    return a, b, (rest - b.astype(F32)).astype(BF16)


def dot(a, b):
    return jnp.dot(a, b, preferred_element_type=F32)


def pack_kernel(k, v, q, o, g, lse, own, copies):
    own[:ROWS] = q[...]
    own[ROWS : 2 * ROWS] = g[...]
    delta = jnp.sum((g[...] * o[...]).T, axis=0, keepdims=True)
    own[2 * ROWS :] = jnp.concatenate([lse[...], delta, jnp.zeros((6, D), F32)], 0)
    for b in range(BLOCKS):
        copies[b, :ROWS] = k[...]
        copies[b, ROWS:] = v[...]


def pack(query, keys, values, attn_out, out_grad, row_lse):
    return pl.pallas_call(pack_kernel, out_shape=[shape(PACK, D), shape(BLOCKS, 2 * ROWS, D)])(
        keys, values, query, attn_out, out_grad, row_lse
    )


def load_block(x_ref, base, factor, row_at, row_factor, at, turned, wide):
    x = x_ref[base : base + ROWS, :] * factor
    high, low = split(x)
    wide[at, :D] = high
    wide[at, D : 2 * D] = high
    wide[at, 2 * D : 3 * D] = low
    high, low = split(x.T)
    turned[:D, at] = high
    turned[D:, at] = low
    a, b, c = split3(x_ref[row_at : row_at + 1, :] * -row_factor)
    sub = lax.broadcasted_iota(jnp.int32, (D, ROWS), 0)
    tail = jnp.where(sub == 0, a.astype(F32), jnp.where(sub == 1, b.astype(F32), jnp.where(sub == 2, c.astype(F32), 0.0)))
    wide[at, 3 * D :] = tail.T.astype(BF16)


def tile_kernel(*refs):
    packs, kv_ref, mine, theirs, dkv_ref = refs[:BLOCKS], *refs[BLOCKS : BLOCKS + 4]
    q_turned, g_turned, q_all, g_all, dq = refs[BLOCKS + 4 :]
    step = pl.program_id(0)

    @pl.when(step == 0)
    def _():
        for b in range(BLOCKS):
            at = slice(b * ROWS, (b + 1) * ROWS)
            load_block(packs[b], 0, SCALE * LOG2E, 2 * ROWS, LOG2E, at, q_turned, q_all)
            load_block(packs[b], ROWS, 1.0, 2 * ROWS + 1, 1.0, at, g_turned, g_all)
        dq[...] = jnp.zeros_like(dq)

    ones = (lax.broadcasted_iota(jnp.int32, (D, TK), 0) < 3).astype(F32).astype(BF16)
    k = kv_ref[:, :ROWS, :].reshape(TK, D)
    v = kv_ref[:, ROWS:, :].reshape(TK, D)
    k_high, k_low = split(k.T)
    v_high, v_low = split(v.T)
    k_all = jnp.concatenate([k_high, k_low, k_high, ones], 0)
    v_all = jnp.concatenate([v_high, v_low, v_high, ones], 0)
    k_wide = jnp.concatenate(split(k), 1)
    dvt = jnp.zeros((D, TK), F32)
    dkt = jnp.zeros((D, TK), F32)
    for j in range(TOKENS // TQ):
        at = slice(j * TQ, (j + 1) * TQ)
        probs = jnp.exp2(dot(q_all[at, :], k_all))
        dprob = dot(g_all[at, :], v_all)
        high, low = split(probs)
        part = dot(g_turned[:, at], high)
        dvt += part[:D] + part[D:] + dot(g_turned[:D, at], low)
        high, low = split(probs * dprob)
        part = dot(q_turned[:, at], high)
        dkt += part[:D] + part[D:] + dot(q_turned[:D, at], low)
        part = dot(high, k_wide) + dot(low, k_wide)
        dq[at, :] = dq[at, :] + (part[:, :D] + part[:, D:])
    dkv_ref[:, :ROWS, :] = (dkt * LN2).T.reshape(TK // ROWS, ROWS, D)
    dkv_ref[:, ROWS:, :] = dvt.T.reshape(TK // ROWS, ROWS, D)

    @pl.when(step == pl.num_programs(0) - 1)
    def _():
        for j in range(CHUNKS):
            for b in range(2):
                at = (4 * j + b) * ROWS
                mine[j, b] = dq[at : at + ROWS] * SCALE
                at += 2 * ROWS
                theirs[j, b] = dq[at : at + ROWS] * SCALE


def tile_grads(packs, kv):
    half = (CHUNKS, 2, ROWS, D)
    block = pl.BlockSpec((TK // ROWS, 2 * ROWS, D), lambda i: (i, 0, 0))
    return pl.pallas_call(
        tile_kernel,
        grid=(TOKENS // TK,),
        in_specs=[pl.BlockSpec((PACK, D), lambda i: (0, 0))] * BLOCKS + [block],
        out_specs=[pl.BlockSpec(half, lambda i: (0, 0, 0, 0))] * 2 + [block],
        out_shape=[shape(*half), shape(*half), pltpu.HBM((BLOCKS, 2 * ROWS, D), F32)],
        scratch_shapes=[pltpu.VMEM((2 * D, TOKENS), BF16)] * 2
        + [pltpu.VMEM((TOKENS, 4 * D), BF16)] * 2
        + [pltpu.VMEM((TOKENS, D), F32)],
        compiler_params=pltpu.CompilerParams(vmem_limit_bytes=36 * 1024 * 1024),
        cost_estimate=pl.CostEstimate(flops=24_000_000_000, bytes_accessed=8 << 20, transcendentals=TOKENS * TOKENS),
    )(*packs, kv)


def swap(x):
    return lax.ppermute(x, "c", SWAP)


def along(x, step):
    pairs = [(z, (z + step) % DEPTH) for z in range(DEPTH)]
    pairs += [(DEPTH + z, DEPTH + (z - step) % DEPTH) for z in range(DEPTH)]
    return lax.ppermute(x, COLUMN, pairs)


def on_device(query, keys, values, attn_out, out_grad, row_lse):
    own, kv = pack(query, keys, values, attn_out, out_grad, row_lse)
    other = swap(own)
    kv = lax.all_to_all(kv, PLANE, 0, 0)
    a, b = own, other
    packs = []
    for j in range(1, CHUNKS):
        a, b = along(a, 1), along(b, 1)
        packs += [swap(b), swap(a), b, a]
    far = along(a, 1)
    far, *packs = lax.optimization_barrier((far, *packs))
    packs = [pltpu.with_memory_space_constraint(x, pltpu.HBM) for x in [own, other] + packs]
    packs = [packs[0], far, packs[1], swap(far)] + packs[2:]
    mine, theirs, dkv = tile_grads(packs, kv)
    dq = mine + swap(theirs)
    dkv = lax.all_to_all(dkv, PLANE, 0, 0)
    r1 = along(dq[1], 1)
    r2 = along(dq[2], 2)
    r3 = along(dq[3], 3)
    r4 = along(dq[0, 1], 4)
    query_grad = (dq[0, 0] + r4) + (r1[0] + r2[0] + r3[0]) + swap(r1[1] + r2[1] + r3[1])
    query_grad, dkv = lax.optimization_barrier((query_grad, dkv))
    return query_grad, jnp.sum(dkv[:, :ROWS], axis=0), jnp.sum(dkv[:, ROWS:], axis=0)


def solution(mesh):
    fine = Mesh(mesh.devices.reshape(2, 4, 2, 2, DEPTH), AXES)
    rows = P(("xh", "y", "c", "xl", "z"), None)
    cols = P(("xl", "z", "xh", "y", "c"), None)
    return jax.shard_map(
        on_device,
        mesh=fine,
        in_specs=(rows, cols, cols, rows, rows, P(None, ("xh", "y", "c", "xl", "z"))),
        out_specs=(rows, cols, cols),
        check_vma=False,
    )
```

```python
import math

import jax
import jax.numpy as jnp
from jax import lax
from jax.experimental import pallas as pl
from jax.experimental.pallas import tpu as pltpu
from jax.sharding import Mesh, PartitionSpec as P

D = 128
SCALE = 1.0 / math.sqrt(D)
LOG2E = math.log2(math.e)
LN2 = math.log(2.0)
BF16 = jnp.bfloat16
F32 = jnp.float32

AXES = ("xh", "y", "c", "xl", "z")
PLANE = ("xl", "xh", "y")
COLUMN = ("c", "z")
DEPTH = 8
ROWS = 128
BLOCKS = 16
TOKENS = ROWS * BLOCKS
PACK = 2 * ROWS + 8
CHUNKS = 4
TQ = TOKENS // CHUNKS
TK = TOKENS // 2

SWAP = [(0, 1), (1, 0)]


def shape(*dims, dtype=F32):
    return jax.ShapeDtypeStruct(dims, dtype)


def split(x):
    high = x.astype(BF16)
    return high, (x - high.astype(F32)).astype(BF16)


def split3(x):
    a = x.astype(BF16)
    rest = x - a.astype(F32)
    b = rest.astype(BF16)
    return a, b, (rest - b.astype(F32)).astype(BF16)


def dot(a, b):
    return jnp.dot(a, b, preferred_element_type=F32)


def pack_kernel(k, v, q, o, g, lse, own, copies):
    own[:ROWS] = q[...]
    own[ROWS : 2 * ROWS] = g[...]
    delta = jnp.sum((g[...] * o[...]).T, axis=0, keepdims=True)
    own[2 * ROWS :] = jnp.concatenate([lse[...], delta, jnp.zeros((6, D), F32)], 0)
    for b in range(BLOCKS):
        copies[b, :ROWS] = k[...]
        copies[b, ROWS:] = v[...]


def pack(query, keys, values, attn_out, out_grad, row_lse):
    return pl.pallas_call(pack_kernel, out_shape=[shape(PACK, D), shape(BLOCKS, 2 * ROWS, D)])(
        keys, values, query, attn_out, out_grad, row_lse
    )


def load_block(x_ref, base, factor, row_at, row_factor, at, turned, wide):
    x = x_ref[base : base + ROWS, :] * factor
    high, low = split(x)
    wide[at, :D] = high
    wide[at, D : 2 * D] = high
    wide[at, 2 * D : 3 * D] = low
    high, low = split(x.T)
    turned[:D, at] = high
    turned[D:, at] = low
    a, b, c = split3(x_ref[row_at : row_at + 1, :] * -row_factor)
    sub = lax.broadcasted_iota(jnp.int32, (D, ROWS), 0)
    tail = jnp.where(sub == 0, a.astype(F32), jnp.where(sub == 1, b.astype(F32), jnp.where(sub == 2, c.astype(F32), 0.0)))
    wide[at, 3 * D :] = tail.T.astype(BF16)


def tile_kernel(*refs):
    packs, kv_ref, mine, theirs, dkv_ref = refs[:BLOCKS], *refs[BLOCKS : BLOCKS + 4]
    q_turned, g_turned, q_all, g_all, dq = refs[BLOCKS + 4 :]
    step = pl.program_id(0)

    @pl.when(step == 0)
    def _():
        for b in range(BLOCKS):
            at = slice(b * ROWS, (b + 1) * ROWS)
            load_block(packs[b], 0, SCALE * LOG2E, 2 * ROWS, LOG2E, at, q_turned, q_all)
            load_block(packs[b], ROWS, 1.0, 2 * ROWS + 1, 1.0, at, g_turned, g_all)
        dq[...] = jnp.zeros_like(dq)

    ones = (lax.broadcasted_iota(jnp.int32, (D, TK), 0) < 3).astype(F32).astype(BF16)
    k = kv_ref[:, :ROWS, :].reshape(TK, D)
    v = kv_ref[:, ROWS:, :].reshape(TK, D)
    k_high, k_low = split(k.T)
    v_high, v_low = split(v.T)
    k_all = jnp.concatenate([k_high, k_low, k_high, ones], 0)
    v_all = jnp.concatenate([v_high, v_low, v_high, ones], 0)
    k_wide = jnp.concatenate(split(k), 1)
    dvt = jnp.zeros((D, TK), F32)
    dkt = jnp.zeros((D, TK), F32)
    for j in range(TOKENS // TQ):
        at = slice(j * TQ, (j + 1) * TQ)
        probs = jnp.exp2(dot(q_all[at, :], k_all))
        dprob = dot(g_all[at, :], v_all)
        high, low = split(probs)
        part = dot(g_turned[:, at], high)
        dvt += part[:D] + part[D:] + dot(g_turned[:D, at], low)
        high, low = split(probs * dprob)
        part = dot(q_turned[:, at], high)
        dkt += part[:D] + part[D:] + dot(q_turned[:D, at], low)
        part = dot(high, k_wide) + dot(low, k_wide)
        dq[at, :] = dq[at, :] + (part[:, :D] + part[:, D:])
    dkv_ref[:, :ROWS, :] = (dkt * LN2).T.reshape(TK // ROWS, ROWS, D)
    dkv_ref[:, ROWS:, :] = dvt.T.reshape(TK // ROWS, ROWS, D)

    @pl.when(step == pl.num_programs(0) - 1)
    def _():
        for j in range(CHUNKS):
            for b in range(2):
                at = (4 * j + b) * ROWS
                mine[j, b] = dq[at : at + ROWS] * SCALE
                at += 2 * ROWS
                theirs[j, b] = dq[at : at + ROWS] * SCALE


def tile_grads(packs, kv):
    half = (CHUNKS, 2, ROWS, D)
    block = pl.BlockSpec((TK // ROWS, 2 * ROWS, D), lambda i: (i, 0, 0))
    return pl.pallas_call(
        tile_kernel,
        grid=(TOKENS // TK,),
        in_specs=[pl.BlockSpec((PACK, D), lambda i: (0, 0))] * BLOCKS + [block],
        out_specs=[pl.BlockSpec(half, lambda i: (0, 0, 0, 0))] * 2 + [block],
        out_shape=[shape(*half), shape(*half), pltpu.HBM((BLOCKS, 2 * ROWS, D), F32)],
        scratch_shapes=[pltpu.VMEM((2 * D, TOKENS), BF16)] * 2
        + [pltpu.VMEM((TOKENS, 4 * D), BF16)] * 2
        + [pltpu.VMEM((TOKENS, D), F32)],
        compiler_params=pltpu.CompilerParams(vmem_limit_bytes=36 * 1024 * 1024),
        cost_estimate=pl.CostEstimate(flops=24_000_000_000, bytes_accessed=8 << 20, transcendentals=TOKENS * TOKENS),
    )(*packs, kv)


def swap(x):
    return lax.ppermute(x, "c", SWAP)


def along(x, step):
    pairs = [(z, (z + step) % DEPTH) for z in range(DEPTH)]
    pairs += [(DEPTH + z, DEPTH + (z - step) % DEPTH) for z in range(DEPTH)]
    return lax.ppermute(x, COLUMN, pairs)


def across(x):
    pairs = [(DEPTH + z, (z + 1) % DEPTH) for z in range(DEPTH)]
    pairs += [(z, DEPTH + (z - 1) % DEPTH) for z in range(DEPTH)]
    return lax.ppermute(x, COLUMN, pairs)


def on_device(query, keys, values, attn_out, out_grad, row_lse):
    own, kv = pack(query, keys, values, attn_out, out_grad, row_lse)
    kv = lax.all_to_all(kv, PLANE, 0, 0)
    other = swap(own)
    a, b = along(own, 1), across(own)
    packs = [own, other, swap(b), swap(a), b, a]
    for _ in range(2, CHUNKS):
        a, b = along(a, 1), along(b, 1)
        packs += [swap(b), swap(a), b, a]
    far = along(a, 1)
    far_other = along(b, 1)
    packs = [pltpu.with_memory_space_constraint(x, pltpu.HBM) for x in packs]
    packs = [packs[0], far, packs[1], far_other] + packs[2:]
    mine, theirs, dkv = tile_grads(packs, kv)
    dq = mine + swap(theirs)
    dkv = lax.all_to_all(dkv, PLANE, 0, 0)
    r1 = along(dq[1], 1)
    r2 = along(dq[2], 2)
    r3 = along(dq[3], 3)
    r4 = along(dq[0, 1], 4)
    query_grad = (dq[0, 0] + r4) + (r1[0] + r2[0] + r3[0]) + swap(r1[1] + r2[1] + r3[1])
    query_grad, dkv = lax.optimization_barrier((query_grad, dkv))
    return query_grad, jnp.sum(dkv[:, :ROWS], axis=0), jnp.sum(dkv[:, ROWS:], axis=0)


def solution(mesh):
    fine = Mesh(mesh.devices.reshape(2, 4, 2, 2, DEPTH), AXES)
    rows = P(("xh", "y", "c", "xl", "z"), None)
    cols = P(("xl", "z", "xh", "y", "c"), None)
    return jax.shard_map(
        on_device,
        mesh=fine,
        in_specs=(rows, cols, cols, rows, rows, P(None, ("xh", "y", "c", "xl", "z"))),
        out_specs=(rows, cols, cols),
        check_vma=False,
    )
```

```python
import math

import jax
import jax.numpy as jnp
from jax import lax
from jax.experimental import pallas as pl
from jax.experimental.pallas import tpu as pltpu
from jax.sharding import Mesh, PartitionSpec as P

D = 128
SCALE = 1.0 / math.sqrt(D)
LOG2E = math.log2(math.e)
LN2 = math.log(2.0)
BF16 = jnp.bfloat16
F32 = jnp.float32

AXES = ("xh", "y", "c", "xl", "z")
PLANE = ("xl", "xh", "y")
COLUMN = ("c", "z")
DEPTH = 8
ROWS = 128
BLOCKS = 16
TOKENS = ROWS * BLOCKS
PACK = 2 * ROWS + 8
CHUNKS = 4
TQ = TOKENS // CHUNKS
TK = TOKENS

SWAP = [(0, 1), (1, 0)]


def shape(*dims, dtype=F32):
    return jax.ShapeDtypeStruct(dims, dtype)


def split(x):
    high = x.astype(BF16)
    return high, (x - high.astype(F32)).astype(BF16)


def split3(x):
    a = x.astype(BF16)
    rest = x - a.astype(F32)
    b = rest.astype(BF16)
    return a, b, (rest - b.astype(F32)).astype(BF16)


def dot(a, b):
    return jnp.dot(a, b, preferred_element_type=F32)


def pack_kernel(k, v, q, o, g, lse, own, copies):
    own[:ROWS] = q[...]
    own[ROWS : 2 * ROWS] = g[...]
    delta = jnp.sum((g[...] * o[...]).T, axis=0, keepdims=True)
    own[2 * ROWS :] = jnp.concatenate([lse[...], delta, jnp.zeros((6, D), F32)], 0)
    for b in range(BLOCKS):
        copies[b, :ROWS] = k[...]
        copies[b, ROWS:] = v[...]


def pack(query, keys, values, attn_out, out_grad, row_lse):
    return pl.pallas_call(pack_kernel, out_shape=[shape(PACK, D), shape(BLOCKS, 2 * ROWS, D)])(
        keys, values, query, attn_out, out_grad, row_lse
    )


def load_block(x_ref, base, factor, row_at, row_factor, at, turned, wide):
    x = x_ref[base : base + ROWS, :] * factor
    high, low = split(x)
    wide[at, :D] = high
    wide[at, D : 2 * D] = high
    wide[at, 2 * D : 3 * D] = low
    high, low = split(x.T)
    turned[:D, at] = high
    turned[D:, at] = low
    a, b, c = split3(x_ref[row_at : row_at + 1, :] * -row_factor)
    sub = lax.broadcasted_iota(jnp.int32, (D, ROWS), 0)
    tail = jnp.where(sub == 0, a.astype(F32), jnp.where(sub == 1, b.astype(F32), jnp.where(sub == 2, c.astype(F32), 0.0)))
    wide[at, 3 * D :] = tail.T.astype(BF16)


def tile_kernel(*refs):
    packs, kv_ref, mine, theirs, dkv_ref = refs[:BLOCKS], *refs[BLOCKS : BLOCKS + 4]
    q_turned, g_turned, q_all, g_all, dq = refs[BLOCKS + 4 :]
    step = pl.program_id(0)

    @pl.when(step == 0)
    def _():
        for b in range(BLOCKS):
            at = slice(b * ROWS, (b + 1) * ROWS)
            load_block(packs[b], 0, SCALE * LOG2E, 2 * ROWS, LOG2E, at, q_turned, q_all)
            load_block(packs[b], ROWS, 1.0, 2 * ROWS + 1, 1.0, at, g_turned, g_all)
        dq[...] = jnp.zeros_like(dq)

    ones = (lax.broadcasted_iota(jnp.int32, (D, TK), 0) < 3).astype(F32).astype(BF16)
    k = kv_ref[:, :ROWS, :].reshape(TK, D)
    v = kv_ref[:, ROWS:, :].reshape(TK, D)
    k_high, k_low = split(k.T)
    v_high, v_low = split(v.T)
    k_all = jnp.concatenate([k_high, k_low, k_high, ones], 0)
    v_all = jnp.concatenate([v_high, v_low, v_high, ones], 0)
    k_wide = jnp.concatenate(split(k), 1)
    dvt = jnp.zeros((D, TK), F32)
    dkt = jnp.zeros((D, TK), F32)
    for j in range(TOKENS // TQ):
        at = slice(j * TQ, (j + 1) * TQ)
        probs = jnp.exp2(dot(q_all[at, :], k_all))
        dprob = dot(g_all[at, :], v_all)
        high, low = split(probs)
        part = dot(g_turned[:, at], high)
        dvt += part[:D] + part[D:] + dot(g_turned[:D, at], low)
        high, low = split(probs * dprob)
        part = dot(q_turned[:, at], high)
        dkt += part[:D] + part[D:] + dot(q_turned[:D, at], low)
        part = dot(high, k_wide) + dot(low, k_wide)
        dq[at, :] = dq[at, :] + (part[:, :D] + part[:, D:])
    dkv_ref[:, :ROWS, :] = (dkt * LN2).T.reshape(TK // ROWS, ROWS, D)
    dkv_ref[:, ROWS:, :] = dvt.T.reshape(TK // ROWS, ROWS, D)

    @pl.when(step == pl.num_programs(0) - 1)
    def _():
        for j in range(CHUNKS):
            for b in range(2):
                at = (4 * j + b) * ROWS
                mine[j, b] = dq[at : at + ROWS] * SCALE
                at += 2 * ROWS
                theirs[j, b] = dq[at : at + ROWS] * SCALE


def tile_grads(packs, kv):
    half = (CHUNKS, 2, ROWS, D)
    block = pl.BlockSpec((TK // ROWS, 2 * ROWS, D), lambda i: (i, 0, 0))
    return pl.pallas_call(
        tile_kernel,
        grid=(TOKENS // TK,),
        in_specs=[pl.BlockSpec((PACK, D), lambda i: (0, 0))] * BLOCKS + [block],
        out_specs=[pl.BlockSpec(half, lambda i: (0, 0, 0, 0))] * 2 + [block],
        out_shape=[shape(*half), shape(*half), pltpu.HBM((BLOCKS, 2 * ROWS, D), F32)],
        scratch_shapes=[pltpu.VMEM((2 * D, TOKENS), BF16)] * 2
        + [pltpu.VMEM((TOKENS, 4 * D), BF16)] * 2
        + [pltpu.VMEM((TOKENS, D), F32)],
        compiler_params=pltpu.CompilerParams(vmem_limit_bytes=48 * 1024 * 1024),
        cost_estimate=pl.CostEstimate(flops=24_000_000_000, bytes_accessed=8 << 20, transcendentals=TOKENS * TOKENS),
    )(*packs, kv)


def swap(x):
    return lax.ppermute(x, "c", SWAP)


def along(x, step):
    pairs = [(z, (z + step) % DEPTH) for z in range(DEPTH)]
    pairs += [(DEPTH + z, DEPTH + (z - step) % DEPTH) for z in range(DEPTH)]
    return lax.ppermute(x, COLUMN, pairs)


def across(x):
    pairs = [(DEPTH + z, (z + 1) % DEPTH) for z in range(DEPTH)]
    pairs += [(z, DEPTH + (z - 1) % DEPTH) for z in range(DEPTH)]
    return lax.ppermute(x, COLUMN, pairs)


def on_device(query, keys, values, attn_out, out_grad, row_lse):
    own, kv = pack(query, keys, values, attn_out, out_grad, row_lse)
    kv = lax.all_to_all(kv, PLANE, 0, 0)
    other = swap(own)
    a, b = along(own, 1), across(own)
    packs = [own, other, swap(b), swap(a), b, a]
    for _ in range(2, CHUNKS):
        a, b = along(a, 1), along(b, 1)
        packs += [swap(b), swap(a), b, a]
    far = along(a, 1)
    far_other = along(b, 1)
    packs = [pltpu.with_memory_space_constraint(x, pltpu.HBM) for x in packs]
    packs = [packs[0], far, packs[1], far_other] + packs[2:]
    mine, theirs, dkv = tile_grads(packs, kv)
    dq = mine + swap(theirs)
    dkv = lax.all_to_all(dkv, PLANE, 0, 0)
    r1 = along(dq[1], 1)
    r2 = along(dq[2], 2)
    r3 = along(dq[3], 3)
    r4 = along(dq[0, 1], 4)
    query_grad = (dq[0, 0] + r4) + (r1[0] + r2[0] + r3[0]) + swap(r1[1] + r2[1] + r3[1])
    query_grad, dkv = lax.optimization_barrier((query_grad, dkv))
    return query_grad, jnp.sum(dkv[:, :ROWS], axis=0), jnp.sum(dkv[:, ROWS:], axis=0)


def solution(mesh):
    fine = Mesh(mesh.devices.reshape(2, 4, 2, 2, DEPTH), AXES)
    rows = P(("xh", "y", "c", "xl", "z"), None)
    cols = P(("xl", "z", "xh", "y", "c"), None)
    return jax.shard_map(
        on_device,
        mesh=fine,
        in_specs=(rows, cols, cols, rows, rows, P(None, ("xh", "y", "c", "xl", "z"))),
        out_specs=(rows, cols, cols),
        check_vma=False,
    )
```

```python
import math

import jax
import jax.numpy as jnp
from jax import lax
from jax.experimental import pallas as pl
from jax.experimental.pallas import tpu as pltpu
from jax.sharding import Mesh, PartitionSpec as P

D = 128
SCALE = 1.0 / math.sqrt(D)
LOG2E = math.log2(math.e)
LN2 = math.log(2.0)
BF16 = jnp.bfloat16
F32 = jnp.float32

AXES = ("xh", "y", "c", "xl", "z")
PLANE = ("xl", "xh", "y")
COLUMN = ("c", "z")
DEPTH = 8
ROWS = 128
BLOCKS = 16
TOKENS = ROWS * BLOCKS
PACK = 2 * ROWS + 8
CHUNKS = 4
TQ = TOKENS // CHUNKS
TK = TOKENS

SWAP = [(0, 1), (1, 0)]


def shape(*dims, dtype=F32):
    return jax.ShapeDtypeStruct(dims, dtype)


def split(x):
    high = x.astype(BF16)
    return high, (x - high.astype(F32)).astype(BF16)


def split3(x):
    a = x.astype(BF16)
    rest = x - a.astype(F32)
    b = rest.astype(BF16)
    return a, b, (rest - b.astype(F32)).astype(BF16)


def dot(a, b):
    return jnp.dot(a, b, preferred_element_type=F32)


def pack_kernel(k, v, q, o, g, lse, own, copies):
    own[:ROWS] = q[...]
    own[ROWS : 2 * ROWS] = g[...]
    delta = jnp.sum((g[...] * o[...]).T, axis=0, keepdims=True)
    own[2 * ROWS :] = jnp.concatenate([lse[...], delta, jnp.zeros((6, D), F32)], 0)
    for b in range(BLOCKS):
        copies[b, :ROWS] = k[...]
        copies[b, ROWS:] = v[...]


def pack(query, keys, values, attn_out, out_grad, row_lse):
    return pl.pallas_call(pack_kernel, out_shape=[shape(PACK, D), shape(BLOCKS, 2 * ROWS, D)])(
        keys, values, query, attn_out, out_grad, row_lse
    )


def load_block(x_ref, base, factor, row_at, row_factor, at, turned, wide):
    x = x_ref[base : base + ROWS, :] * factor
    high, low = split(x)
    wide[at, :D] = high
    wide[at, D : 2 * D] = high
    wide[at, 2 * D : 3 * D] = low
    high, low = split(x.T)
    turned[:D, at] = high
    turned[D:, at] = low
    a, b, c = split3(x_ref[row_at : row_at + 1, :] * -row_factor)
    sub = lax.broadcasted_iota(jnp.int32, (D, ROWS), 0)
    tail = jnp.where(sub == 0, a.astype(F32), jnp.where(sub == 1, b.astype(F32), jnp.where(sub == 2, c.astype(F32), 0.0)))
    wide[at, 3 * D :] = tail.T.astype(BF16)


def tile_kernel(*refs):
    packs, kv_any, mine, theirs, dkv_any = refs[:BLOCKS], *refs[BLOCKS : BLOCKS + 4]
    q_turned, g_turned, q_all, g_all, kv_ref, dk_ref, dv_ref, sems = refs[BLOCKS + 4 :]
    fetch = pltpu.make_async_copy(kv_any, kv_ref, sems.at[0])
    dk_out = pltpu.make_async_copy(dk_ref, dkv_any.at[:, :ROWS, :], sems.at[1])
    dv_out = pltpu.make_async_copy(dv_ref, dkv_any.at[:, ROWS:, :], sems.at[2])
    fetch.start()

    for b in range(BLOCKS):
        at = slice(b * ROWS, (b + 1) * ROWS)
        load_block(packs[b], 0, SCALE * LOG2E, 2 * ROWS, LOG2E, at, q_turned, q_all)
        load_block(packs[b], ROWS, 1.0, 2 * ROWS + 1, 1.0, at, g_turned, g_all)

    fetch.wait()
    ones = (lax.broadcasted_iota(jnp.int32, (D, TK), 0) < 3).astype(F32).astype(BF16)
    k = kv_ref[:, :ROWS, :].reshape(TK, D)
    v = kv_ref[:, ROWS:, :].reshape(TK, D)
    k_high, k_low = split(k.T)
    v_high, v_low = split(v.T)
    k_all = jnp.concatenate([k_high, k_low, k_high, ones], 0)
    v_all = jnp.concatenate([v_high, v_low, v_high, ones], 0)
    k_wide = jnp.concatenate(split(k), 1)
    dvt = jnp.zeros((D, TK), F32)
    dkt = jnp.zeros((D, TK), F32)
    for j in range(TOKENS // TQ):
        at = slice(j * TQ, (j + 1) * TQ)
        probs = jnp.exp2(dot(q_all[at, :], k_all))
        dprob = dot(g_all[at, :], v_all)
        high, low = split(probs)
        part = dot(g_turned[:, at], high)
        dvt += part[:D] + part[D:] + dot(g_turned[:D, at], low)
        if j == TOKENS // TQ - 1:
            dv_ref[...] = dvt.T.reshape(BLOCKS, ROWS, D)
            dv_out.start()
        high, low = split(probs * dprob)
        part = dot(q_turned[:, at], high)
        dkt += part[:D] + part[D:] + dot(q_turned[:D, at], low)
        part = dot(high, k_wide) + dot(low, k_wide)
        part = (part[:, :D] + part[:, D:]) * SCALE
        for b in range(2):
            mine[j, b] = part[b * ROWS : (b + 1) * ROWS]
            theirs[j, b] = part[(b + 2) * ROWS : (b + 3) * ROWS]
    dk_ref[...] = (dkt * LN2).T.reshape(BLOCKS, ROWS, D)
    dk_out.start()
    dv_out.wait()
    dk_out.wait()


def tile_grads(packs, kv):
    half = (CHUNKS, 2, ROWS, D)
    block = pl.BlockSpec(memory_space=pl.ANY)
    return pl.pallas_call(
        tile_kernel,
        grid=(TOKENS // TK,),
        in_specs=[pl.BlockSpec((PACK, D), lambda i: (0, 0))] * BLOCKS + [block],
        out_specs=[pl.BlockSpec(half, lambda i: (0, 0, 0, 0))] * 2 + [block],
        out_shape=[shape(*half), shape(*half), pltpu.HBM((BLOCKS, 2 * ROWS, D), F32)],
        scratch_shapes=[pltpu.VMEM((2 * D, TOKENS), BF16)] * 2
        + [pltpu.VMEM((TOKENS, 4 * D), BF16)] * 2
        + [pltpu.VMEM((BLOCKS, 2 * ROWS, D), F32)]
        + [pltpu.VMEM((BLOCKS, ROWS, D), F32)] * 2
        + [pltpu.SemaphoreType.DMA((3,))],
        compiler_params=pltpu.CompilerParams(vmem_limit_bytes=48 * 1024 * 1024),
        cost_estimate=pl.CostEstimate(flops=24_000_000_000, bytes_accessed=8 << 20, transcendentals=TOKENS * TOKENS),
    )(*packs, kv)


def swap(x):
    return lax.ppermute(x, "c", SWAP)


def along(x, step):
    pairs = [(z, (z + step) % DEPTH) for z in range(DEPTH)]
    pairs += [(DEPTH + z, DEPTH + (z - step) % DEPTH) for z in range(DEPTH)]
    return lax.ppermute(x, COLUMN, pairs)


def across(x):
    pairs = [(DEPTH + z, (z + 1) % DEPTH) for z in range(DEPTH)]
    pairs += [(z, DEPTH + (z - 1) % DEPTH) for z in range(DEPTH)]
    return lax.ppermute(x, COLUMN, pairs)


def on_device(query, keys, values, attn_out, out_grad, row_lse):
    own, kv = pack(query, keys, values, attn_out, out_grad, row_lse)
    kv = lax.all_to_all(kv, PLANE, 0, 0)
    other = swap(own)
    a, b = along(own, 1), across(own)
    packs = [own, other, swap(b), swap(a), b, a]
    for _ in range(2, CHUNKS):
        a, b = along(a, 1), along(b, 1)
        packs += [swap(b), swap(a), b, a]
    far = along(a, 1)
    far_other = along(b, 1)
    packs = [pltpu.with_memory_space_constraint(x, pltpu.HBM) for x in packs]
    packs = [packs[0], far, packs[1], far_other] + packs[2:]
    mine, theirs, dkv = tile_grads(packs, kv)
    dq = mine + swap(theirs)
    dkv = lax.all_to_all(dkv, PLANE, 0, 0)
    r1 = along(dq[1], 1)
    r2 = along(dq[2], 2)
    r3 = along(dq[3], 3)
    r4 = along(dq[0, 1], 4)
    query_grad = (dq[0, 0] + r4) + (r1[0] + r2[0] + r3[0]) + swap(r1[1] + r2[1] + r3[1])
    query_grad, dkv = lax.optimization_barrier((query_grad, dkv))
    return query_grad, jnp.sum(dkv[:, :ROWS], axis=0), jnp.sum(dkv[:, ROWS:], axis=0)


def solution(mesh):
    fine = Mesh(mesh.devices.reshape(2, 4, 2, 2, DEPTH), AXES)
    rows = P(("xh", "y", "c", "xl", "z"), None)
    cols = P(("xl", "z", "xh", "y", "c"), None)
    return jax.shard_map(
        on_device,
        mesh=fine,
        in_specs=(rows, cols, cols, rows, rows, P(None, ("xh", "y", "c", "xl", "z"))),
        out_specs=(rows, cols, cols),
        check_vma=False,
    )
```
